128 devices in a mesh: section: 4 (over x_hi, core), replica: 4 (over z), tensor: 8 (over y, x_lo).
Axes of the slice: x: 4 (x_hi: 2, x_lo: 2; x = x_hi * 2 + x_lo), y: 4, z: 4, core: 2. Of those that a mesh axis runs over, the one named last changes fastest.
Arguments:
- out_grad: bfloat16 [4, 8, 128, 1024], P('replica', None, 'tensor'), may hold values from -6 to 6
- relu_mask: int32 [4, 4, 8, 128, 4096], P('section', 'replica', None, None, 'tensor'), may hold values from 0 to 255
- w_in: bfloat16 [4, 1024, 32768], P('section', None, 'tensor'), may hold values from -0.1875 to 0.1875
- w_out: bfloat16 [4, 32768, 1024], P('section', 'tensor'), may hold values from -0.03125 to 0.03125
- route: int32 [3, 8, 4], replicated, may hold values from 0 to 3, each once within a row
Outputs:
- in_grads: bfloat16 [4, 4, 8, 128, 1024], P('section', 'replica', None, 'tensor')
The draws below stay inside these ranges and needn't reach their ends.
Inputs may be any that keep to these rules, and one draw needn't show every extreme that they name: Each route[s, m, :] is a permutation of the replicas.
All inputs are finite; a program needn't handle non-finite values.
Results may differ from the reference program's by a relative error of at most 0.0095.
Values may be sent and summed in bfloat16 or wider, within the bound.
No kernel may reach another device: no remote copies, remote signals or barrier semaphores. Data moves between devices by JAX's collectives and lax.ppermute only.
A program may use at most 128 MiB of HBM per device.

```python
import jax
import jax.numpy as jnp

D = 1024
FF = 32768
MB = 128
MICRO = 8
WORDS = 4096
N_SECTION = 4
N_REPLICA = 4


def touch_ends(result, key, smallest, high):
    spot = [jax.random.randint(jax.random.fold_in(key, axis), (), 0, length) for axis, length in enumerate(result.shape)]
    main_axis = result.shape.index(max(result.shape))
    neighbour = spot[:main_axis] + [(spot[main_axis] + 1) % result.shape[main_axis]] + spot[main_axis + 1:]
    return result.at[tuple(spot)].set(smallest).at[tuple(neighbour)].set(high)


def shard_levels(own_key, shape, cuts, least, high):
    factor_of, own = 1.0, jax.random.fold_in(own_key, 6)
    for axis_at, blocks in cuts:
        heights = jnp.exp(jax.random.uniform(jax.random.fold_in(own, axis_at), (blocks,), jnp.float32, least / len(cuts), high / len(cuts)))
        factor_of = factor_of * jnp.repeat(heights, shape[axis_at] // blocks).reshape([-1 if axis == axis_at else 1 for axis in range(len(shape))])
    return factor_of


def noise(rng, shape, scale, limit, pieces=(), kind=jnp.bfloat16):
    entries = scale * jax.random.normal(rng, shape, jnp.float32)
    if pieces:
        entries = entries * shard_levels(rng, shape, pieces, -0.22, 0.18)
    return jnp.clip(entries, -limit, limit).astype(kind)


def setup_inputs(seed: int = 0) -> dict:
    splits = jax.random.split(jax.random.key(seed), 6)
    return {
        "out_grad": noise(splits[0], (N_REPLICA, MICRO, MB, D), 1.0, 6.0, ((0, 4), (2, 8))),
        "relu_mask": touch_ends(jax.random.randint(splits[1], (N_SECTION, N_REPLICA, MICRO, MB, WORDS), 0, 256), jax.random.fold_in(splits[1], 1), 0, 255).astype(jnp.int32),
        "w_in": noise(splits[2], (N_SECTION, D, FF), D ** -0.5, 0.1875, ((0, 4), (2, 8))),
        "w_out": noise(splits[3], (N_SECTION, FF, D), FF ** -0.5, 0.03125, ((0, 4), (1, 8))),
        "route": jax.vmap(lambda own: jax.random.permutation(own, N_REPLICA))(jax.random.split(splits[4], (N_SECTION - 1) * MICRO)).reshape((N_SECTION - 1, MICRO, N_REPLICA)).astype(jnp.int32),
    }


def unpack_bits(words):
    shifts = jnp.arange(8, dtype=jnp.int32)
    bits = jnp.right_shift(words[..., None], shifts) & 1
    return bits.reshape(words.shape[:-1] + (words.shape[-1] * 8,))


def reference(out_grad, relu_mask, w_in, w_out, route):
    incoming = out_grad
    results = []
    for section in reversed(range(N_SECTION)):
        flat = incoming.reshape(-1, D)
        pre = jnp.dot(flat, w_out[section].T, preferred_element_type=jnp.float32)
        masked = unpack_bits(relu_mask[section].reshape(-1, WORDS))
        hidden = jnp.where(masked != 0, pre, jnp.float32(0.0)).astype(jnp.bfloat16)
        term = jnp.dot(hidden, w_in[section].T, preferred_element_type=jnp.float32)
        grads = (flat.astype(jnp.float32) + term).astype(jnp.bfloat16).reshape(incoming.shape)
        results.append(grads)
        if section > 0:
            table = route[section - 1]
            slots = jnp.arange(N_REPLICA, dtype=jnp.int32)
            onehot = (table[:, :, None] == slots[None, None, :]).astype(jnp.float32)
            incoming = jnp.einsum("msq,smnd->qmnd", onehot, grads.astype(jnp.float32)).astype(jnp.bfloat16)
    return jnp.stack(results[::-1])
```

```python
import functools

import jax
import jax.numpy as jnp
from jax import lax
from jax.experimental import pallas as pl
from jax.experimental.pallas import tpu as pltpu
from jax.sharding import PartitionSpec as P

CHUNK = 4
LAG = 1
BLOCK = 1024


def block_kernel(chunk_ref, x_ref, w_out_ref, w_in_ref, mask_ref, out_ref, acc_ref, spread_ref):
    step = pl.program_id(0)
    parts, rows = x_ref.shape[0], x_ref.shape[1]
    micro = mask_ref.shape[0]
    tokens = rows // micro

    @pl.when(step == 0)
    def _():
        word = lax.broadcasted_iota(jnp.int32, spread_ref.shape, 0)
        unit = lax.broadcasted_iota(jnp.int32, spread_ref.shape, 1)
        spread_ref[...] = jnp.where(
            jnp.right_shift(unit, 3) == word, jnp.float32(1), jnp.float32(0)
        ).astype(jnp.bfloat16)

    x = x_ref[...].reshape(parts * rows, x_ref.shape[2])
    pre = lax.dot_general(
        x, w_out_ref[...], (((1,), (1,)), ((), ())), preferred_element_type=jnp.float32
    )
    words = jnp.concatenate(
        [mask_ref[m, t * tokens : (t + 1) * tokens, :] for t in range(parts) for m in range(micro)],
        axis=0,
    )
    words = words.astype(jnp.float32).astype(jnp.bfloat16)
    spread = jnp.dot(words, spread_ref[...], preferred_element_type=jnp.float32).astype(jnp.int32)
    unit = lax.broadcasted_iota(jnp.int32, (1, BLOCK), 1)
    bit = jnp.left_shift(jnp.int32(1), jnp.bitwise_and(unit, 7))
    hidden = jnp.where(jnp.bitwise_and(spread, bit) != 0, pre, jnp.float32(0)).astype(jnp.bfloat16)
    term = lax.dot_general(
        hidden, w_in_ref[...], (((1,), (1,)), ((), ())), preferred_element_type=jnp.float32
    )

    @pl.when(step == 0)
    def _():
        acc_ref[...] = term

    @pl.when(step > 0)
    def _():
        acc_ref[...] += term

    @pl.when(step == pl.num_programs(0) - 1)
    def _():
        out_ref[...] = acc_ref[...].astype(jnp.bfloat16).reshape(out_ref.shape)


def block_sums(chunk, x, w_out, w_in, masks):
    parts, rows, width = x.shape
    units = w_out.shape[0]
    words = BLOCK // 8
    total = parts * rows
    spec = pltpu.PrefetchScalarGridSpec(
        num_scalar_prefetch=1,
        grid=(units // BLOCK,),
        in_specs=[
            pl.BlockSpec((parts, rows, width), lambda h, c: (0, 0, 0)),
            pl.BlockSpec((BLOCK, width), lambda h, c: (h, 0)),
            pl.BlockSpec((width, BLOCK), lambda h, c: (0, h)),
            pl.BlockSpec((CHUNK, masks.shape[1], words), lambda h, c: (c[0], 0, h)),
        ],
        out_specs=pl.BlockSpec((parts, rows, width), lambda h, c: (0, 0, 0)),
        scratch_shapes=[
            pltpu.VMEM((total, width), jnp.float32),
            pltpu.VMEM((words, BLOCK), jnp.bfloat16),
        ],
    )
    return pl.pallas_call(
        block_kernel,
        grid_spec=spec,
        out_shape=jax.ShapeDtypeStruct((parts, rows, width), jnp.bfloat16),
        compiler_params=pltpu.CompilerParams(vmem_limit_bytes=48 * 1024 * 1024),
        cost_estimate=pl.CostEstimate(
            flops=4 * total * width * units,
            bytes_accessed=4 * width * units + 4 * total * width,
            transcendentals=0,
        ),
    )(chunk.reshape(1), x, w_out, w_in, masks)


def shards(out_grad, relu_mask, w_in, w_out, route):
    n_section = lax.axis_size("section")
    n_replica = lax.axis_size("replica")
    n_tensor = lax.axis_size("tensor")
    micro, tokens, width = out_grad.shape[1:]
    section = lax.axis_index("section")
    replica = lax.axis_index("replica")
    n_chunk = micro // CHUNK
    slots = n_chunk + LAG * (n_section - 1)
    w_in_local, w_out_local, masks = w_in[0], w_out[0], relu_mask[0, 0]
    entry = out_grad[0].reshape(n_chunk, CHUNK * tokens, width)
    results = jnp.zeros((n_chunk, CHUNK * tokens, width), jnp.bfloat16)
    last = n_section - 1
    onward = lax.dynamic_index_in_dim(route, jnp.maximum(section - 1, 0), 0, keepdims=False)
    onward = lax.dynamic_index_in_dim(onward, replica, 1, keepdims=False).reshape(n_chunk, CHUNK)
    carried = {}
    for slot in range(slots):
        offset = slot - LAG * (last - section)
        active = (offset >= 0) & (offset < n_chunk)
        chunk = jnp.clip(offset, 0, n_chunk - 1)
        rows = lax.dynamic_index_in_dim(entry, chunk, 0, keepdims=False)
        if slot in carried:
            rows = jnp.where(section == last, rows, carried.pop(slot))
        everyone = jnp.broadcast_to(rows[None], (n_tensor,) + rows.shape)
        x = lax.all_to_all(everyone, "tensor", 0, 0)
        partial = block_sums(chunk, x, w_out_local, w_in_local, masks)
        pieces = lax.all_to_all(partial, "tensor", 0, 0)
        grads = (
            rows.astype(jnp.float32) + jnp.sum(pieces.astype(jnp.float32), axis=0)
        ).astype(jnp.bfloat16)
        if slot < LAG * last:
            results = jnp.where(
                active, lax.dynamic_update_index_in_dim(results, grads, chunk, 0), results
            )
        else:
            previous = lax.dynamic_index_in_dim(results, chunk, 0, keepdims=False)
            results = lax.dynamic_update_index_in_dim(
                results, jnp.where(active, grads, previous), chunk, 0
            )
        if slot + LAG < slots:
            goes = lax.dynamic_index_in_dim(onward, chunk, 0, keepdims=False)
            here = goes[None, :] == jnp.arange(n_replica, dtype=jnp.int32)[:, None]
            by_micro = grads.reshape(CHUNK, tokens, width)
            out = jnp.where(here[:, :, None, None], by_micro[None], jnp.bfloat16(0))
            got = lax.all_to_all(out, "replica", 0, 0)
            mine = jnp.sum(got.astype(jnp.float32), axis=0).astype(jnp.bfloat16)
            carried[slot + LAG] = lax.ppermute(
                mine.reshape(rows.shape), "section", [(s, s - 1) for s in range(1, n_section)]
            )
    return results.reshape(1, 1, micro, tokens, width)


def solution(mesh):
    in_specs = (
        P("replica", None, "tensor", None),
        P("section", "replica", None, None, "tensor"),
        P("section", None, "tensor"),
        P("section", "tensor", None),
        P(),
    )
    out_specs = P("section", "replica", None, "tensor", None)
    return jax.shard_map(shards, mesh=mesh, in_specs=in_specs, out_specs=out_specs, check_vma=False)
```

```python
import functools

import jax
import jax.numpy as jnp
from jax import lax
from jax.experimental import pallas as pl
from jax.experimental.pallas import tpu as pltpu
from jax.sharding import PartitionSpec as P

N_CHUNK = 2
BLOCK = 1024
GROUP = BLOCK // 8
MIB = 1024 * 1024
LAST_DIMS = (((1,), (1,)), ((), ()))
SCALARS = pl.BlockSpec(memory_space=pltpu.SMEM)
WHOLE = pl.BlockSpec(memory_space=pltpu.VMEM)
OUTSIDE = pl.BlockSpec(memory_space=pltpu.HBM)


def turn(section, slot, n_section):
    offset = slot - (n_section - 1 - section)
    return jnp.clip(offset, 0, N_CHUNK - 1), (offset >= 0) & (offset < N_CHUNK)


def prepare_kernel(slot, n_section, facts_ref, entry_ref, *refs):
    out_ref = refs[-1]
    rows = entry_ref[turn(facts_ref[0], slot, n_section)[0]]
    if len(refs) == 2:
        rows = jnp.where(facts_ref[0] == n_section - 1, rows, refs[0][...])
    out_ref[...] = jnp.broadcast_to(rows[None], out_ref.shape)


def prepare(slot, n_section, parts, facts, entry, carried):
    return pl.pallas_call(
        functools.partial(prepare_kernel, slot, n_section),
        in_specs=[SCALARS] + [WHOLE] * (1 + len(carried)),
        out_specs=WHOLE,
        out_shape=jax.ShapeDtypeStruct((parts,) + entry.shape[1:], entry.dtype),
        compiler_params=pltpu.CompilerParams(vmem_limit_bytes=8 * MIB),
    )(facts, entry, *carried)


def expand_kernel(chunk, n_section, facts_ref, words_ref, out_ref, held_ref, ones_ref, spread_ref, sems):
    sources, micro = words_ref.shape[:2]
    parts, rows = out_ref.shape[:2]
    tokens = rows // micro
    is_last = facts_ref[0] == n_section - 1

    @pl.when(is_last if sources == 1 else jnp.logical_not(is_last))
    def _():
        def read(m):
            source = 0 if sources == 1 else facts_ref[1 + chunk * micro + m]
            return pltpu.make_async_copy(words_ref.at[source, m], held_ref.at[m], sems.at[0, m])

        def write(m):
            place = pl.ds(m * tokens, tokens)
            return pltpu.make_async_copy(
                ones_ref.at[:, place], out_ref.at[:, place], sems.at[1, m]
            )

        for m in range(micro):
            read(m).start()
        word = lax.broadcasted_iota(jnp.int32, spread_ref.shape, 0)
        unit = lax.broadcasted_iota(jnp.int32, spread_ref.shape, 1)
        spread_ref[...] = jnp.where(
            jnp.right_shift(unit, 3) == word, jnp.float32(1), jnp.float32(0)
        ).astype(jnp.bfloat16)
        lane = lax.broadcasted_iota(jnp.int32, (1, BLOCK), 1)
        bit = jnp.left_shift(jnp.int32(1), jnp.bitwise_and(lane, 7))
        for m in range(micro):
            read(m).wait()
            for at in range(held_ref.shape[2] // GROUP):
                words = held_ref[m, :, at * GROUP : (at + 1) * GROUP]
                value = jnp.dot(words, spread_ref[...], preferred_element_type=jnp.float32)
                on = jnp.bitwise_and(value.astype(jnp.int32), bit) != 0
                ones = jnp.where(on, jnp.float32(1), jnp.float32(0)).astype(jnp.bfloat16)
                ones_ref[:, m * tokens : (m + 1) * tokens, at * BLOCK : (at + 1) * BLOCK] = (
                    ones.reshape(parts, tokens, BLOCK)
                )
            write(m).start()
        for m in range(micro):
            write(m).wait()


def expand(chunk, n_section, parts, facts, words):
    _, micro, tokens, count = words.shape
    shape = (parts, micro * tokens // parts, 8 * count)
    return pl.pallas_call(
        functools.partial(expand_kernel, chunk, n_section),
        in_specs=[SCALARS, OUTSIDE],
        out_specs=OUTSIDE,
        out_shape=jax.ShapeDtypeStruct(shape, jnp.bfloat16),
        scratch_shapes=[
            pltpu.VMEM((micro, tokens, count), jnp.bfloat16),
            pltpu.VMEM(shape, jnp.bfloat16),
            pltpu.VMEM((GROUP, BLOCK), jnp.bfloat16),
            pltpu.SemaphoreType.DMA((2, micro)),
        ],
        compiler_params=pltpu.CompilerParams(vmem_limit_bytes=56 * MIB),
        cost_estimate=pl.CostEstimate(
            flops=micro * tokens * count * 8 * 512,
            bytes_accessed=micro * tokens * count * 18,
            transcendentals=0,
        ),
    )(facts, words)


def block_kernel(slot, n_section, holders, facts_ref, x_ref, w_out_ref, w_in_ref, *refs):
    *mask_refs, out_ref, w_out_buf, w_in_buf, mask_buf, acc_ref, sems = refs
    parts, rows, width = x_ref.shape
    total = parts * rows
    blocks = w_out_ref.shape[0] // BLOCK

    def mask(at, act):
        units = pl.ds(at * BLOCK, BLOCK)
        for holder, ref in zip(holders, mask_refs):
            copy = pltpu.make_async_copy(
                ref.at[:, :, units], mask_buf.at[:, :, units], sems.at[2, at]
            )
            if len(holders) == 1:
                act(copy)
            else:

                @pl.when(facts_ref[0] == holder)
                def _(copy=copy):
                    act(copy)

    def first(at):
        units = pl.ds(at * BLOCK, BLOCK)
        return pltpu.make_async_copy(w_out_ref.at[units], w_out_buf.at[units], sems.at[0, at])

    def second(at):
        units = pl.ds(at * BLOCK, BLOCK)
        return pltpu.make_async_copy(w_in_ref.at[:, units], w_in_buf.at[:, units], sems.at[1, at])

    def hidden(at):
        units = pl.ds(at * BLOCK, BLOCK)
        pre = lax.dot_general(
            x_ref[...].reshape(total, width),
            w_out_buf[units, :],
            LAST_DIMS,
            preferred_element_type=jnp.float32,
        )
        return pre.astype(jnp.bfloat16) * mask_buf[:, :, units].reshape(total, BLOCK)

    for at in range(blocks):
        first(at).start()
        mask(at, lambda copy: copy.start())
        second(at).start()
    first(0).wait()
    mask(0, lambda copy: copy.wait())
    now = hidden(0)
    for at in range(blocks):
        units = pl.ds(at * BLOCK, BLOCK)
        second(at).wait()
        if at < blocks - 1:
            first(at + 1).wait()
            mask(at + 1, lambda copy: copy.wait())
        term = lax.dot_general(
            now, w_in_buf[:, units], LAST_DIMS, preferred_element_type=jnp.float32
        )
        if at < blocks - 1:
            now = hidden(at + 1)
        if at == 0:
            acc_ref[...] = term
        elif at < blocks - 1:
            acc_ref[...] += term
        else:
            out_ref[...] = (acc_ref[...] + term).astype(jnp.bfloat16).reshape(out_ref.shape)


def block_sums(slot, n_section, facts, x, w_out, w_in, masks):
    parts, rows, width = x.shape
    total = parts * rows
    units = w_out.shape[0]
    return pl.pallas_call(
        functools.partial(block_kernel, slot, n_section, tuple(masks)),
        in_specs=[SCALARS, WHOLE] + [OUTSIDE] * (2 + len(masks)),
        out_specs=WHOLE,
        out_shape=jax.ShapeDtypeStruct((parts, rows, width), jnp.bfloat16),
        scratch_shapes=[
            pltpu.VMEM((units, width), jnp.bfloat16),
            pltpu.VMEM((width, units), jnp.bfloat16),
            pltpu.VMEM((parts, rows, units), jnp.bfloat16),
            pltpu.VMEM((total, width), jnp.float32),
            pltpu.SemaphoreType.DMA((3, units // BLOCK)),
        ],
        compiler_params=pltpu.CompilerParams(vmem_limit_bytes=52 * MIB),
        cost_estimate=pl.CostEstimate(
            flops=4 * total * width * units, bytes_accessed=4 * width * units, transcendentals=0
        ),
    )(facts, x, w_out, w_in, *masks.values())


def address_kernel(n_section, facts_ref, *refs):
    *grads_refs, out_ref = refs
    n_replica, micro, tokens, _ = out_ref.shape
    per_chunk = micro // N_CHUNK
    for chunk in range(N_CHUNK):
        for section in range(n_section):

            @pl.when(facts_ref[0] == section)
            def _(chunk=chunk, section=section):
                value = grads_refs[chunk + n_section - 1 - section]
                for i in range(per_chunk):
                    m = chunk * per_chunk + i
                    rows = value[i * tokens : (i + 1) * tokens, :]
                    for q in range(n_replica):
                        mine = jnp.where(facts_ref[1 + m] == q, rows, jnp.zeros_like(rows))
                        out_ref[q, m] = mine


def address(n_section, n_replica, micro, facts, grads):
    rows, width = grads[0].shape
    return pl.pallas_call(
        functools.partial(address_kernel, n_section),
        in_specs=[SCALARS] + [WHOLE] * len(grads),
        out_specs=WHOLE,
        out_shape=jax.ShapeDtypeStruct((n_replica, micro, rows * N_CHUNK // micro, width), jnp.bfloat16),
        compiler_params=pltpu.CompilerParams(vmem_limit_bytes=8 * MIB),
    )(facts, *grads)


def shards(out_grad, relu_mask, w_in, w_out, route):
    n_section = lax.axis_size("section")
    n_replica = lax.axis_size("replica")
    n_tensor = lax.axis_size("tensor")
    micro, tokens, width = out_grad.shape[1:]
    section = lax.axis_index("section")
    replica = lax.axis_index("replica")
    per_chunk = micro // N_CHUNK
    last = n_section - 1
    slots = N_CHUNK + last
    w_in_local, w_out_local = w_in[0], w_out[0]
    entry = out_grad[0].reshape(N_CHUNK, per_chunk * tokens, width)
    names = jnp.arange(n_replica, dtype=jnp.int32)

    belongs = jnp.broadcast_to(replica, (micro,)).astype(jnp.int32)
    for hop in range(last - 1, -1, -1):
        moved = jnp.sum(jnp.where(belongs[:, None] == names, route[hop], 0), axis=1)
        belongs = jnp.where(section <= hop, moved, belongs)
    facts = jnp.concatenate([section.astype(jnp.int32).reshape(1), belongs])

    def words_of(mask, at):
        return mask[0, 0, at * per_chunk : (at + 1) * per_chunk].astype(jnp.bfloat16)

    def swap(value):
        return lax.all_to_all(value, "tensor", 0, 0)

    def work(slot, rows, everyone, masks):
        x = swap(everyone)
        partial = block_sums(slot, n_section, facts, x, w_out_local, w_in_local, masks)
        total = jnp.sum(swap(partial).astype(jnp.float32), axis=0)
        return (rows.astype(jnp.float32) + total).astype(jnp.bfloat16)

    words = [words_of(relu_mask, 0)]
    gathered = [lax.all_gather(words[0], "replica", axis=0)]
    own, got, carried, grads = [], [], [], []
    for slot in range(slots):
        active = turn(section, slot, n_section)[1]
        if slot == 0:

            def start(relu_mask, entry):
                everyone = jnp.broadcast_to(entry[:1], (n_tensor,) + entry.shape[1:])
                own = [
                    expand(at, n_section, n_tensor, facts, words_of(relu_mask, at)[None])
                    for at in range(N_CHUNK)
                ]
                return work(0, entry[0], everyone, {last: own[0]}), own[1]

            def rest(relu_mask, entry):
                shape = (n_tensor, per_chunk * tokens, w_out_local.shape[0])
                return entry[0], jnp.zeros(shape, jnp.bfloat16)

            result, own = lax.cond(active, start, rest, relu_mask, entry)
        else:
            if slot < 1 + N_CHUNK:
                at = slot - 1
                got.append(expand(at, n_section, n_tensor, facts, gathered[at]))
            masks = {}
            for holder in range(last + 1):
                chunk = slot - (last - holder)
                if 0 <= chunk < N_CHUNK:
                    masks[holder] = own if holder == last else got[chunk]
            everyone = prepare(slot, n_section, n_tensor, facts, entry, carried)
            result = lax.cond(
                active,
                lambda everyone, *values: work(
                    slot, everyone[0], everyone, dict(zip(masks, values))
                ),
                lambda everyone, *values: everyone[0],
                everyone,
                *masks.values(),
            )
        grads.append(result)
        if slot < slots - 1:
            hops = [(s, s - 1) for s in range(1, n_section)]
            carried = [lax.ppermute(result, "section", hops)]
        if slot == 0:
            for at in range(1, N_CHUNK):
                later, _ = lax.optimization_barrier((relu_mask, result))
                gathered.append(lax.all_gather(words_of(later, at), "replica", axis=0))
    outgoing = address(n_section, n_replica, micro, facts, grads)
    got = lax.all_to_all(outgoing, "replica", 0, 0)
    done = jnp.sum(got.astype(jnp.float32), axis=0).astype(jnp.bfloat16)
    return done[None, None]


def solution(mesh):
    in_specs = (
        P("replica", None, "tensor", None),
        P("section", "replica", None, None, "tensor"),
        P("section", None, "tensor"),
        P("section", "tensor", None),
        P(),
    )
    out_specs = P("section", "replica", None, "tensor", None)
    return jax.shard_map(shards, mesh=mesh, in_specs=in_specs, out_specs=out_specs, check_vma=False)
```

```python
import functools

import jax
import jax.numpy as jnp
from jax import lax
from jax.experimental import pallas as pl
from jax.experimental.pallas import tpu as pltpu
from jax.sharding import PartitionSpec as P

N_CHUNK = 2
BLOCK = 1024
GROUP = BLOCK // 8
MIB = 1024 * 1024
LAST_DIMS = (((1,), (1,)), ((), ()))
SCALARS = pl.BlockSpec(memory_space=pltpu.SMEM)
WHOLE = pl.BlockSpec(memory_space=pltpu.VMEM)
OUTSIDE = pl.BlockSpec(memory_space=pltpu.HBM)


def turn(section, slot, n_section):
    offset = slot - (n_section - 1 - section)
    return jnp.clip(offset, 0, N_CHUNK - 1), (offset >= 0) & (offset < N_CHUNK)


def prepare_kernel(slot, n_section, facts_ref, entry_ref, *refs):
    out_ref = refs[-1]
    rows = entry_ref[turn(facts_ref[0], slot, n_section)[0]]
    if len(refs) == 2:
        rows = jnp.where(facts_ref[0] == n_section - 1, rows, refs[0][...])
    out_ref[...] = jnp.broadcast_to(rows[None], out_ref.shape)


def prepare(slot, n_section, parts, facts, entry, carried):
    return pl.pallas_call(
        functools.partial(prepare_kernel, slot, n_section),
        in_specs=[SCALARS] + [WHOLE] * (1 + len(carried)),
        out_specs=WHOLE,
        out_shape=jax.ShapeDtypeStruct((parts,) + entry.shape[1:], entry.dtype),
        compiler_params=pltpu.CompilerParams(vmem_limit_bytes=8 * MIB),
    )(facts, entry, *carried)


def expand_kernel(chunk, facts_ref, words_ref, out_ref, held_ref, ones_ref, spread_ref, sems):
    sources = words_ref.shape[0]
    micro = held_ref.shape[0]
    parts, rows = out_ref.shape[:2]
    tokens = rows // micro

    def read(m):
        at = chunk * micro + m
        source = 0 if sources == 1 else facts_ref[1 + at]
        return pltpu.make_async_copy(words_ref.at[source, at], held_ref.at[m], sems.at[0, m])

    def write(m):
        place = pl.ds(pl.multiple_of(m * tokens, tokens), tokens)
        return pltpu.make_async_copy(ones_ref.at[m], out_ref.at[:, place], sems.at[1, m])

    for m in range(micro):
        read(m).start()
    word = lax.broadcasted_iota(jnp.int32, spread_ref.shape, 0)
    unit = lax.broadcasted_iota(jnp.int32, spread_ref.shape, 1)
    spread_ref[...] = jnp.where(
        jnp.right_shift(unit, 3) == word, jnp.float32(1), jnp.float32(0)
    ).astype(jnp.bfloat16)
    lane = lax.broadcasted_iota(jnp.int32, (1, BLOCK), 1)
    bit = jnp.left_shift(jnp.int32(1), jnp.bitwise_and(lane, 7))

    @pl.loop(0, micro)
    def _(m):
        read(m).wait()
        for at in range(held_ref.shape[2] // GROUP):
            words = held_ref[m, :, at * GROUP : (at + 1) * GROUP]
            value = jnp.dot(words, spread_ref[...], preferred_element_type=jnp.float32)
            on = jnp.bitwise_and(value.astype(jnp.int32), bit) != 0
            ones = jnp.where(on, jnp.float32(1), jnp.float32(0)).astype(jnp.bfloat16)
            ones_ref[m, :, :, at * BLOCK : (at + 1) * BLOCK] = ones.reshape(parts, tokens, BLOCK)
        write(m).start()

    for m in range(micro):
        write(m).wait()


def expand(chunk, parts, facts, words):
    _, micro, tokens, count = words.shape
    micro //= N_CHUNK
    shape = (parts, micro * tokens // parts, 8 * count)
    return pl.pallas_call(
        functools.partial(expand_kernel, chunk),
        in_specs=[SCALARS, OUTSIDE],
        out_specs=OUTSIDE,
        out_shape=jax.ShapeDtypeStruct(shape, jnp.bfloat16),
        scratch_shapes=[
            pltpu.VMEM((micro, tokens, count), jnp.bfloat16),
            pltpu.VMEM((micro, parts, tokens // parts, 8 * count), jnp.bfloat16),
            pltpu.VMEM((GROUP, BLOCK), jnp.bfloat16),
            pltpu.SemaphoreType.DMA((2, micro)),
        ],
        compiler_params=pltpu.CompilerParams(vmem_limit_bytes=56 * MIB),
        cost_estimate=pl.CostEstimate(
            flops=micro * tokens * count * 8 * 512,
            bytes_accessed=micro * tokens * count * 18,
            transcendentals=0,
        ),
    )(facts, words)


def block_kernel(holders, x_outside, facts_ref, x_ref, w_out_ref, w_in_ref, *refs):
    mask_refs, refs = refs[: len(holders)], refs[len(holders) :]
    out_ref, w_out_buf, w_in_buf, mask_buf, acc_ref, sems = refs[:6]
    parts, rows, width = x_ref.shape
    total = parts * rows
    blocks = w_out_ref.shape[0] // BLOCK
    x_buf = refs[6] if x_outside else x_ref

    def place(at):
        start = at * BLOCK
        return pl.ds(start if isinstance(at, int) else pl.multiple_of(start, BLOCK), BLOCK)

    def weights(at):
        units = place(at)
        return (
            pltpu.make_async_copy(w_out_ref.at[units], w_out_buf.at[units], sems.at[at, 0]),
            pltpu.make_async_copy(w_in_ref.at[:, units], w_in_buf.at[:, units], sems.at[at, 1]),
        )

    def mask(at, ref):
        units = place(at)
        return pltpu.make_async_copy(ref.at[:, :, units], mask_buf.at[:, :, units], sems.at[at, 2])

    if x_outside:
        x_copy = pltpu.make_async_copy(x_ref, x_buf, sems.at[blocks, 0])
        x_copy.start()
    for at in range(blocks):
        first, second = weights(at)
        first.start()
        if len(holders) == 1:
            mask(at, mask_refs[0]).start()
        else:
            for holder, ref in zip(holders, mask_refs):

                @pl.when(facts_ref[0] == holder)
                def _(at=at, ref=ref):
                    mask(at, ref).start()

        second.start()
    if x_outside:
        x_copy.wait()

    def step(at):
        units = place(at)
        first, second = weights(at)
        first.wait()
        mask(at, mask_refs[0]).wait()
        second.wait()
        pre = lax.dot_general(
            x_buf[...].reshape(total, width),
            w_out_buf[units, :],
            LAST_DIMS,
            preferred_element_type=jnp.float32,
        )
        hidden = pre.astype(jnp.bfloat16) * mask_buf[:, :, units].reshape(total, BLOCK)
        return lax.dot_general(
            hidden, w_in_buf[:, units], LAST_DIMS, preferred_element_type=jnp.float32
        )

    acc_ref[...] = jnp.zeros_like(acc_ref)

    @pl.loop(0, blocks)
    def _(at):
        acc_ref[...] += step(at)

    out_ref[...] = acc_ref[...].astype(jnp.bfloat16).reshape(out_ref.shape)


def block_sums(facts, x, w_out, w_in, masks, x_outside):
    parts, rows, width = x.shape
    total = parts * rows
    units = w_out.shape[0]
    scratch = [
        pltpu.VMEM((units, width), jnp.bfloat16),
        pltpu.VMEM((width, units), jnp.bfloat16),
        pltpu.VMEM((parts, rows, units), jnp.bfloat16),
        pltpu.VMEM((total, width), jnp.float32),
        pltpu.SemaphoreType.DMA((units // BLOCK + 1, 3)),
    ]
    if x_outside:
        scratch.append(pltpu.VMEM((parts, rows, width), jnp.bfloat16))
    return pl.pallas_call(
        functools.partial(block_kernel, tuple(masks), x_outside),
        in_specs=[SCALARS, OUTSIDE if x_outside else WHOLE] + [OUTSIDE] * (2 + len(masks)),
        out_specs=WHOLE,
        out_shape=jax.ShapeDtypeStruct((parts, rows, width), jnp.bfloat16),
        scratch_shapes=scratch,
        compiler_params=pltpu.CompilerParams(vmem_limit_bytes=52 * MIB),
        cost_estimate=pl.CostEstimate(
            flops=4 * total * width * units, bytes_accessed=4 * width * units, transcendentals=0
        ),
    )(facts, x, w_out, w_in, *masks.values())


def address_kernel(n_section, facts_ref, *refs):
    *grads_refs, out_ref = refs
    n_replica, micro, tokens, _ = out_ref.shape
    per_chunk = micro // N_CHUNK
    for chunk in range(N_CHUNK):
        for section in range(n_section):

            @pl.when(facts_ref[0] == section)
            def _(chunk=chunk, section=section):
                value = grads_refs[chunk + n_section - 1 - section]
                for i in range(per_chunk):
                    m = chunk * per_chunk + i
                    rows = value[i * tokens : (i + 1) * tokens, :]
                    for q in range(n_replica):
                        mine = jnp.where(facts_ref[1 + m] == q, rows, jnp.zeros_like(rows))
                        out_ref[q, m] = mine


def address(n_section, n_replica, micro, facts, grads):
    rows, width = grads[0].shape
    return pl.pallas_call(
        functools.partial(address_kernel, n_section),
        in_specs=[SCALARS] + [WHOLE] * len(grads),
        out_specs=WHOLE,
        out_shape=jax.ShapeDtypeStruct((n_replica, micro, rows * N_CHUNK // micro, width), jnp.bfloat16),
        compiler_params=pltpu.CompilerParams(vmem_limit_bytes=8 * MIB),
    )(facts, *grads)


def shards(out_grad, relu_mask, w_in, w_out, route):
    n_section = lax.axis_size("section")
    n_replica = lax.axis_size("replica")
    n_tensor = lax.axis_size("tensor")
    micro, tokens, width = out_grad.shape[1:]
    section = lax.axis_index("section")
    replica = lax.axis_index("replica")
    per_chunk = micro // N_CHUNK
    last = n_section - 1
    slots = N_CHUNK + last
    w_in_local, w_out_local = w_in[0], w_out[0]
    entry = out_grad[0].reshape(N_CHUNK, per_chunk * tokens, width)
    names = jnp.arange(n_replica, dtype=jnp.int32)

    def facts_of(route):
        belongs = jnp.broadcast_to(replica, (micro,)).astype(jnp.int32)
        for hop in range(last - 1, -1, -1):
            moved = jnp.sum(jnp.where(belongs[:, None] == names, route[hop], 0), axis=1)
            belongs = jnp.where(section <= hop, moved, belongs)
        return jnp.concatenate([section.astype(jnp.int32).reshape(1), belongs])

    def swap(value):
        return lax.all_to_all(value, "tensor", 0, 0)

    def work(facts, everyone, masks, x_outside=False):
        x = swap(everyone)
        partial = block_sums(facts, x, w_out_local, w_in_local, masks, x_outside)
        total = jnp.sum(swap(partial).astype(jnp.float32), axis=0)
        return (everyone[0].astype(jnp.float32) + total).astype(jnp.bfloat16)

    def expand_all(facts, words):
        return [expand(at, n_tensor, facts, words) for at in range(N_CHUNK)]

    def start(entry, relu_mask, route):
        everyone = jnp.broadcast_to(entry[:1], (n_tensor,) + entry.shape[1:])
        nothing = jnp.zeros((1,), jnp.int32)
        masks = expand_all(nothing, relu_mask[0].astype(jnp.bfloat16))
        return [work(nothing, everyone, {last: masks[0]}, True)] + masks

    def rest(entry, relu_mask, route):
        words = relu_mask[0, 0].astype(jnp.bfloat16)
        copies = jnp.broadcast_to(words[None], (n_replica,) + words.shape)
        masks = expand_all(facts_of(route), lax.all_to_all(copies, "replica", 0, 0))
        return [entry[0]] + masks

    carried, grads = [], []
    for slot in range(slots):
        active = turn(section, slot, n_section)[1]
        holders = {}
        for holder in range(last + 1):
            chunk = slot - (last - holder)
            if 0 <= chunk < N_CHUNK:
                holders[holder] = chunk
        if slot == 0:
            result, *masks = lax.cond(active, start, rest, entry, relu_mask, route)
            route, _ = lax.optimization_barrier((route, result))
            facts = facts_of(route)
        else:
            everyone = prepare(slot, n_section, n_tensor, facts, entry, carried)
            result = lax.cond(
                active,
                lambda everyone, *masks: work(
                    facts, everyone, {holder: masks[chunk] for holder, chunk in holders.items()}
                ),
                lambda everyone, *masks: everyone[0],
                everyone,
                *masks,
            )
        grads.append(result)
        if slot < slots - 1:
            carried = [lax.ppermute(result, "section", [(s, s - 1) for s in holders if s > 0])]
    outgoing = address(n_section, n_replica, micro, facts, grads)
    got = lax.all_to_all(outgoing, "replica", 0, 0)
    done = jnp.sum(got.astype(jnp.float32), axis=0).astype(jnp.bfloat16)
    return done[None, None]


def solution(mesh):
    in_specs = (
        P("replica", None, "tensor", None),
        P("section", "replica", None, None, "tensor"),
        P("section", None, "tensor"),
        P("section", "tensor", None),
        P(),
    )
    out_specs = P("section", "replica", None, "tensor", None)
    return jax.shard_map(shards, mesh=mesh, in_specs=in_specs, out_specs=out_specs, check_vma=False)
```

```python
import functools

import jax
import jax.numpy as jnp
from jax import lax
from jax.experimental import pallas as pl
from jax.experimental.pallas import tpu as pltpu
from jax.sharding import PartitionSpec as P

N_CHUNK = 2
BLOCK = 1024
COLUMNS = 512
GROUP = BLOCK // 8
MIB = 1024 * 1024
LAST_DIMS = (((1,), (1,)), ((), ()))
SCALARS = pl.BlockSpec(memory_space=pltpu.SMEM)
WHOLE = pl.BlockSpec(memory_space=pltpu.VMEM)
OUTSIDE = pl.BlockSpec(memory_space=pltpu.HBM)


def turn(section, slot, n_section):
    offset = slot - (n_section - 1 - section)
    return jnp.clip(offset, 0, N_CHUNK - 1), (offset >= 0) & (offset < N_CHUNK)


def expand_kernel(chunk, facts_ref, words_ref, out_ref, held_ref, ones_ref, spread_ref, sems):
    sources = words_ref.shape[0]
    micro = held_ref.shape[0]
    parts, rows = out_ref.shape[:2]
    tokens = rows // micro

    def read(m):
        at = chunk * micro + m
        source = 0 if sources == 1 else facts_ref[1 + at]
        return pltpu.make_async_copy(words_ref.at[source, at], held_ref.at[m], sems.at[0, m])

    def write(m):
        place = pl.ds(pl.multiple_of(m * tokens, tokens), tokens)
        return pltpu.make_async_copy(ones_ref.at[m], out_ref.at[:, place], sems.at[1, m])

    for m in range(micro):
        read(m).start()
    word = lax.broadcasted_iota(jnp.int32, spread_ref.shape, 0)
    unit = lax.broadcasted_iota(jnp.int32, spread_ref.shape, 1)
    spread_ref[...] = jnp.where(
        jnp.right_shift(unit, 3) == word, jnp.float32(1), jnp.float32(0)
    ).astype(jnp.bfloat16)
    lane = lax.broadcasted_iota(jnp.int32, (1, BLOCK), 1)
    bit = jnp.left_shift(jnp.int32(1), jnp.bitwise_and(lane, 7))

    @pl.loop(0, micro)
    def _(m):
        read(m).wait()
        for at in range(held_ref.shape[2] // GROUP):
            words = held_ref[m, :, at * GROUP : (at + 1) * GROUP]
            value = jnp.dot(words, spread_ref[...], preferred_element_type=jnp.float32)
            on = jnp.bitwise_and(value.astype(jnp.int32), bit) != 0
            ones = jnp.where(on, jnp.float32(1), jnp.float32(0)).astype(jnp.bfloat16)
            ones_ref[m, :, :, at * BLOCK : (at + 1) * BLOCK] = ones.reshape(parts, tokens, BLOCK)
        write(m).start()

    for m in range(micro):
        write(m).wait()


def expand(chunk, parts, facts, words):
    _, micro, tokens, count = words.shape
    micro //= N_CHUNK
    shape = (parts, micro * tokens // parts, 8 * count)
    return pl.pallas_call(
        functools.partial(expand_kernel, chunk),
        in_specs=[SCALARS, OUTSIDE],
        out_specs=OUTSIDE,
        out_shape=jax.ShapeDtypeStruct(shape, jnp.bfloat16),
        scratch_shapes=[
            pltpu.VMEM((micro, tokens, count), jnp.bfloat16),
            pltpu.VMEM((micro, parts, tokens // parts, 8 * count), jnp.bfloat16),
            pltpu.VMEM((GROUP, BLOCK), jnp.bfloat16),
            pltpu.SemaphoreType.DMA((2, micro)),
        ],
        compiler_params=pltpu.CompilerParams(vmem_limit_bytes=56 * MIB),
        cost_estimate=pl.CostEstimate(
            flops=micro * tokens * count * 8 * 512,
            bytes_accessed=micro * tokens * count * 18,
            transcendentals=0,
        ),
    )(facts, words)


def block_kernel(holders, facts_ref, x_ref, w_out_ref, w_in_ref, *refs):
    mask_refs, refs = refs[: len(holders)], refs[len(holders) :]
    out_ref, w_out_buf, w_in_buf, mask_buf, hidden_ref, sems = refs
    parts, rows, width = x_ref.shape
    total = parts * rows
    n_up, n_down = w_out_ref.shape[0] // BLOCK, width // COLUMNS

    def place(at, size):
        return pl.ds(at * size if isinstance(at, int) else pl.multiple_of(at * size, size), size)

    def up(at):
        units = place(at, BLOCK)
        return pltpu.make_async_copy(w_out_ref.at[units], w_out_buf.at[units], sems.at[0, at])

    def mask(at, ref):
        units = place(at, BLOCK)
        return pltpu.make_async_copy(ref.at[:, :, units], mask_buf.at[:, :, units], sems.at[1, at])

    def down(at):
        columns = place(at, COLUMNS)
        return pltpu.make_async_copy(w_in_ref.at[columns], w_in_buf.at[columns], sems.at[2, at])

    for at in range(n_up):
        up(at).start()
        if len(holders) == 1:
            mask(at, mask_refs[0]).start()
        else:
            for holder, ref in zip(holders, mask_refs):

                @pl.when(facts_ref[0] == holder)
                def _(at=at, ref=ref):
                    mask(at, ref).start()

    for at in range(n_down):
        down(at).start()

    @pl.loop(0, n_up)
    def _(at):
        up(at).wait()
        mask(at, mask_refs[0]).wait()
        units = place(at, BLOCK)
        pre = lax.dot_general(
            x_ref[...].reshape(total, width),
            w_out_buf[units, :],
            LAST_DIMS,
            preferred_element_type=jnp.float32,
        )
        hidden_ref[:, units] = pre.astype(jnp.bfloat16) * mask_buf[:, :, units].reshape(total, BLOCK)

    @pl.loop(0, n_down)
    def _(at):
        down(at).wait()
        columns = place(at, COLUMNS)
        term = lax.dot_general(
            hidden_ref[...], w_in_buf[columns, :], LAST_DIMS, preferred_element_type=jnp.float32
        )
        out_ref[:, :, columns] = term.astype(jnp.bfloat16).reshape(parts, rows, COLUMNS)


def block_sums(facts, x, w_out, w_in, masks):
    parts, rows, width = x.shape
    total = parts * rows
    units = w_out.shape[0]
    return pl.pallas_call(
        functools.partial(block_kernel, tuple(masks)),
        in_specs=[SCALARS, WHOLE] + [OUTSIDE] * (2 + len(masks)),
        out_specs=WHOLE,
        out_shape=jax.ShapeDtypeStruct((parts, rows, width), jnp.bfloat16),
        scratch_shapes=[
            pltpu.VMEM((units, width), jnp.bfloat16),
            pltpu.VMEM((width, units), jnp.bfloat16),
            pltpu.VMEM((parts, rows, units), jnp.bfloat16),
            pltpu.VMEM((total, units), jnp.bfloat16),
            pltpu.SemaphoreType.DMA((3, max(units // BLOCK, width // COLUMNS))),
        ],
        compiler_params=pltpu.CompilerParams(vmem_limit_bytes=52 * MIB),
        cost_estimate=pl.CostEstimate(
            flops=4 * total * width * units, bytes_accessed=4 * width * units, transcendentals=0
        ),
    )(facts, x, w_out, w_in, *masks.values())


def address_kernel(n_section, facts_ref, *refs):
    *grads_refs, out_ref = refs
    n_replica, micro, tokens, _ = out_ref.shape
    per_chunk = micro // N_CHUNK
    for chunk in range(N_CHUNK):
        for section in range(n_section):

            @pl.when(facts_ref[0] == section)
            def _(chunk=chunk, section=section):
                value = grads_refs[chunk + n_section - 1 - section]
                for i in range(per_chunk):
                    m = chunk * per_chunk + i
                    rows = value[i * tokens : (i + 1) * tokens, :]
                    for q in range(n_replica):
                        mine = jnp.where(facts_ref[1 + m] == q, rows, jnp.zeros_like(rows))
                        out_ref[q, m] = mine


def address(n_section, n_replica, micro, facts, grads):
    rows, width = grads[0].shape
    return pl.pallas_call(
        functools.partial(address_kernel, n_section),
        in_specs=[SCALARS] + [WHOLE] * len(grads),
        out_specs=WHOLE,
        out_shape=jax.ShapeDtypeStruct((n_replica, micro, rows * N_CHUNK // micro, width), jnp.bfloat16),
        compiler_params=pltpu.CompilerParams(vmem_limit_bytes=8 * MIB),
    )(facts, *grads)


def shards(out_grad, relu_mask, w_in, w_out, route):
    n_section = lax.axis_size("section")
    n_replica = lax.axis_size("replica")
    n_tensor = lax.axis_size("tensor")
    micro, tokens, width = out_grad.shape[1:]
    section = lax.axis_index("section")
    replica = lax.axis_index("replica")
    per_chunk = micro // N_CHUNK
    last = n_section - 1
    slots = N_CHUNK + last
    w_in_local, w_out_local = w_in[0], w_out[0]
    entry = out_grad[0].reshape(N_CHUNK, per_chunk * tokens, width)
    names = jnp.arange(n_replica, dtype=jnp.int32)

    def facts_of(route):
        belongs = jnp.broadcast_to(replica, (micro,)).astype(jnp.int32)
        for hop in range(last - 1, -1, -1):
            moved = jnp.sum(jnp.where(belongs[:, None] == names, route[hop], 0), axis=1)
            belongs = jnp.where(section <= hop, moved, belongs)
        return jnp.concatenate([section.astype(jnp.int32).reshape(1), belongs])

    def swap(value):
        return lax.all_to_all(value, "tensor", 0, 0)

    def work(facts, rows, masks):
        x = swap(jnp.broadcast_to(rows[None], (n_tensor,) + rows.shape))
        partial = block_sums(facts, x, w_out_local, w_in_local, masks)
        total = jnp.sum(swap(partial).astype(jnp.float32), axis=0)
        return (rows.astype(jnp.float32) + total).astype(jnp.bfloat16)

    def expand_all(facts, words):
        return [expand(at, n_tensor, facts, words) for at in range(N_CHUNK)]

    def start(entry, relu_mask, route):
        facts = jnp.where(jnp.arange(1 + micro) == 0, section, replica).astype(jnp.int32)
        masks = expand_all(facts, relu_mask[0].astype(jnp.bfloat16))
        return [work(facts, entry[0], {last: masks[0]}), facts] + masks

    def rest(entry, relu_mask, route):
        words = relu_mask[0, 0].astype(jnp.bfloat16)
        copies = jnp.broadcast_to(words[None], (n_replica,) + words.shape)
        facts = facts_of(route)
        return [entry[0], facts] + expand_all(facts, lax.all_to_all(copies, "replica", 0, 0))

    grads = []
    for slot in range(slots):
        active = turn(section, slot, n_section)[1]
        holders = {}
        for holder in range(last + 1):
            chunk = slot - (last - holder)
            if 0 <= chunk < N_CHUNK:
                holders[holder] = chunk
        if slot == 0:
            result, facts, *masks = lax.cond(active, start, rest, entry, relu_mask, route)
        else:
            rows = carried
            if last in holders:
                rows = jnp.where(section == last, entry[holders[last]], rows)
            result = lax.cond(
                active,
                lambda rows, *masks: work(
                    facts, rows, {holder: masks[chunk] for holder, chunk in holders.items()}
                ),
                lambda rows, *masks: rows,
                rows,
                *masks,
            )
        grads.append(result)
        if slot < slots - 1:
            carried = lax.ppermute(result, "section", [(s, s - 1) for s in holders if s > 0])
    outgoing = address(n_section, n_replica, micro, facts, grads)
    got = lax.all_to_all(outgoing, "replica", 0, 0)
    done = jnp.sum(got.astype(jnp.float32), axis=0).astype(jnp.bfloat16)
    return done[None, None]


def solution(mesh):
    in_specs = (
        P("replica", None, "tensor", None),
        P("section", "replica", None, None, "tensor"),
        P("section", None, "tensor"),
        P("section", "tensor", None),
        P(),
    )
    out_specs = P("section", "replica", None, "tensor", None)
    return jax.shard_map(shards, mesh=mesh, in_specs=in_specs, out_specs=out_specs, check_vma=False)
```

```python
import functools

import jax
import jax.numpy as jnp
from jax import lax
from jax.experimental import pallas as pl
from jax.experimental.pallas import tpu as pltpu
from jax.sharding import PartitionSpec as P

N_CHUNK = 2
BLOCK = 1024
COLUMNS = 512
GROUP = BLOCK // 8
MIB = 1024 * 1024
LAST_DIMS = (((1,), (1,)), ((), ()))
SCALARS = pl.BlockSpec(memory_space=pltpu.SMEM)
WHOLE = pl.BlockSpec(memory_space=pltpu.VMEM)
OUTSIDE = pl.BlockSpec(memory_space=pltpu.HBM)


def turn(section, slot, n_section):
    offset = slot - (n_section - 1 - section)
    return jnp.clip(offset, 0, N_CHUNK - 1), (offset >= 0) & (offset < N_CHUNK)


def expand_kernel(chunk, facts_ref, words_ref, out_ref, held_ref, ones_ref, spread_ref, sems):
    sources = words_ref.shape[0]
    micro = held_ref.shape[0]
    parts, rows = out_ref.shape[:2]
    tokens = rows // micro

    def read(m):
        at = chunk * micro + m
        source = 0 if sources == 1 else facts_ref[1 + at]
        return pltpu.make_async_copy(words_ref.at[source, at], held_ref.at[m], sems.at[0, m])

    def write(m):
        place = pl.ds(pl.multiple_of(m * tokens, tokens), tokens)
        return pltpu.make_async_copy(ones_ref.at[m], out_ref.at[:, place], sems.at[1, m])

    for m in range(micro):
        read(m).start()
    word = lax.broadcasted_iota(jnp.int32, spread_ref.shape, 0)
    unit = lax.broadcasted_iota(jnp.int32, spread_ref.shape, 1)
    spread_ref[...] = jnp.where(
        jnp.right_shift(unit, 3) == word, jnp.float32(1), jnp.float32(0)
    ).astype(jnp.bfloat16)
    lane = lax.broadcasted_iota(jnp.int32, (1, BLOCK), 1)
    bit = jnp.left_shift(jnp.int32(1), jnp.bitwise_and(lane, 7))

    @pl.loop(0, micro)
    def _(m):
        read(m).wait()
        for at in range(held_ref.shape[2] // GROUP):
            words = held_ref[m, :, at * GROUP : (at + 1) * GROUP]
            value = jnp.dot(words, spread_ref[...], preferred_element_type=jnp.float32)
            on = jnp.bitwise_and(value.astype(jnp.int32), bit) != 0
            ones = jnp.where(on, jnp.float32(1), jnp.float32(0)).astype(jnp.bfloat16)
            ones_ref[m, :, :, at * BLOCK : (at + 1) * BLOCK] = ones.reshape(parts, tokens, BLOCK)
        write(m).start()

    for m in range(micro):
        write(m).wait()


def expand(chunk, parts, facts, words):
    _, micro, tokens, count = words.shape
    micro //= N_CHUNK
    shape = (parts, micro * tokens // parts, 8 * count)
    return pl.pallas_call(
        functools.partial(expand_kernel, chunk),
        in_specs=[SCALARS, OUTSIDE],
        out_specs=OUTSIDE,
        out_shape=jax.ShapeDtypeStruct(shape, jnp.bfloat16),
        scratch_shapes=[
            pltpu.VMEM((micro, tokens, count), jnp.bfloat16),
            pltpu.VMEM((micro, parts, tokens // parts, 8 * count), jnp.bfloat16),
            pltpu.VMEM((GROUP, BLOCK), jnp.bfloat16),
            pltpu.SemaphoreType.DMA((2, micro)),
        ],
        compiler_params=pltpu.CompilerParams(vmem_limit_bytes=56 * MIB),
        cost_estimate=pl.CostEstimate(
            flops=micro * tokens * count * 8 * 512,
            bytes_accessed=micro * tokens * count * 18,
            transcendentals=0,
        ),
    )(facts, words)


def block_kernel(holders, fetch, facts_ref, x_ref, w_out_ref, w_in_ref, *refs):
    mask_refs, refs = refs[: len(holders)], refs[len(holders) :]
    out_ref, w_out_buf, w_in_buf, mask_buf, hidden_ref, sems = refs[:6]
    rows_buf = refs[6] if fetch else x_ref
    parts, rows, width = x_ref.shape
    total = parts * rows
    n_up, n_down = w_out_ref.shape[0] // BLOCK, width // COLUMNS

    def place(at, size):
        return pl.ds(at * size if isinstance(at, int) else pl.multiple_of(at * size, size), size)

    def up(at):
        units = place(at, BLOCK)
        return pltpu.make_async_copy(w_out_ref.at[units], w_out_buf.at[units], sems.at[0, at])

    def mask(at, ref):
        units = place(at, BLOCK)
        return pltpu.make_async_copy(ref.at[:, :, units], mask_buf.at[:, :, units], sems.at[1, at])

    def down(at):
        columns = place(at, COLUMNS)
        return pltpu.make_async_copy(w_in_ref.at[columns], w_in_buf.at[columns], sems.at[2, at])

    if fetch:
        rows_copy = pltpu.make_async_copy(x_ref, rows_buf, refs[7])
        rows_copy.start()
    for at in range(n_up):
        up(at).start()
        if len(holders) == 1:
            mask(at, mask_refs[0]).start()
        else:
            for holder, ref in zip(holders, mask_refs):

                @pl.when(facts_ref[0] == holder)
                def _(at=at, ref=ref):
                    mask(at, ref).start()

    for at in range(n_down):
        down(at).start()
    if fetch:
        rows_copy.wait()

    @pl.loop(0, n_up)
    def _(at):
        up(at).wait()
        mask(at, mask_refs[0]).wait()
        units = place(at, BLOCK)
        pre = lax.dot_general(
            rows_buf[...].reshape(total, width),
            w_out_buf[units, :],
            LAST_DIMS,
            preferred_element_type=jnp.float32,
        )
        hidden_ref[:, units] = pre.astype(jnp.bfloat16) * mask_buf[:, :, units].reshape(total, BLOCK)

    @pl.loop(0, n_down)
    def _(at):
        down(at).wait()
        columns = place(at, COLUMNS)
        term = lax.dot_general(
            hidden_ref[...], w_in_buf[columns, :], LAST_DIMS, preferred_element_type=jnp.float32
        )
        out_ref[:, :, columns] = term.astype(jnp.bfloat16).reshape(parts, rows, COLUMNS)


def block_sums(facts, x, w_out, w_in, masks, fetch):
    parts, rows, width = x.shape
    total = parts * rows
    units = w_out.shape[0]
    return pl.pallas_call(
        functools.partial(block_kernel, tuple(masks), fetch),
        in_specs=[SCALARS, OUTSIDE if fetch else WHOLE] + [OUTSIDE] * (2 + len(masks)),
        out_specs=WHOLE,
        out_shape=jax.ShapeDtypeStruct((parts, rows, width), jnp.bfloat16),
        scratch_shapes=[
            pltpu.VMEM((units, width), jnp.bfloat16),
            pltpu.VMEM((width, units), jnp.bfloat16),
            pltpu.VMEM((parts, rows, units), jnp.bfloat16),
            pltpu.VMEM((total, units), jnp.bfloat16),
            pltpu.SemaphoreType.DMA((3, max(units // BLOCK, width // COLUMNS))),
        ]
        + [pltpu.VMEM(x.shape, x.dtype), pltpu.SemaphoreType.DMA][: 2 * fetch],
        compiler_params=pltpu.CompilerParams(vmem_limit_bytes=52 * MIB),
        cost_estimate=pl.CostEstimate(
            flops=4 * total * width * units, bytes_accessed=4 * width * units, transcendentals=0
        ),
    )(facts, x, w_out, w_in, *masks.values())


def address_kernel(n_section, facts_ref, *refs):
    *grads_refs, out_ref = refs
    n_replica, micro, tokens, _ = out_ref.shape
    per_chunk = micro // N_CHUNK
    for chunk in range(N_CHUNK):
        for section in range(n_section):

            @pl.when(facts_ref[0] == section)
            def _(chunk=chunk, section=section):
                value = grads_refs[chunk + n_section - 1 - section]
                for i in range(per_chunk):
                    m = chunk * per_chunk + i
                    rows = value[i * tokens : (i + 1) * tokens, :]
                    for q in range(n_replica):
                        mine = jnp.where(facts_ref[1 + m] == q, rows, jnp.zeros_like(rows))
                        out_ref[q, m] = mine


def address(n_section, n_replica, micro, facts, grads):
    rows, width = grads[0].shape
    return pl.pallas_call(
        functools.partial(address_kernel, n_section),
        in_specs=[SCALARS] + [WHOLE] * len(grads),
        out_specs=WHOLE,
        out_shape=jax.ShapeDtypeStruct((n_replica, micro, rows * N_CHUNK // micro, width), jnp.bfloat16),
        compiler_params=pltpu.CompilerParams(vmem_limit_bytes=8 * MIB),
    )(facts, *grads)


def shards(out_grad, relu_mask, w_in, w_out, route):
    n_section = lax.axis_size("section")
    n_replica = lax.axis_size("replica")
    n_tensor = lax.axis_size("tensor")
    micro, tokens, width = out_grad.shape[1:]
    section = lax.axis_index("section")
    replica = lax.axis_index("replica")
    per_chunk = micro // N_CHUNK
    last = n_section - 1
    slots = N_CHUNK + last
    w_in_local, w_out_local = w_in[0], w_out[0]
    entry = out_grad[0].reshape(N_CHUNK, per_chunk * tokens, width)
    names = jnp.arange(n_replica, dtype=jnp.int32)

    def facts_of(route):
        belongs = jnp.broadcast_to(replica, (micro,)).astype(jnp.int32)
        for hop in range(last - 1, -1, -1):
            moved = jnp.sum(jnp.where(belongs[:, None] == names, route[hop], 0), axis=1)
            belongs = jnp.where(section <= hop, moved, belongs)
        return jnp.concatenate([section.astype(jnp.int32).reshape(1), belongs])

    def swap(value):
        return lax.all_to_all(value, "tensor", 0, 0)

    def work(facts, rows, masks, fetch=False):
        x = swap(jnp.broadcast_to(rows[None], (n_tensor,) + rows.shape))
        partial = block_sums(facts, x, w_out_local, w_in_local, masks, fetch)
        total = jnp.sum(swap(partial).astype(jnp.float32), axis=0)
        return (rows.astype(jnp.float32) + total).astype(jnp.bfloat16)

    def expand_all(facts, words):
        return [expand(at, n_tensor, facts, words) for at in range(N_CHUNK)]

    def start(entry, relu_mask, route):
        facts = jnp.where(jnp.arange(1 + micro) == 0, section, replica).astype(jnp.int32)
        masks = expand_all(facts, relu_mask[0].astype(jnp.bfloat16))
        return [work(facts, entry[0], {last: masks[0]}, True), facts] + masks

    def rest(entry, relu_mask, route):
        words = relu_mask[0, 0].astype(jnp.bfloat16)
        copies = jnp.broadcast_to(words[None], (n_replica,) + words.shape)
        facts = facts_of(route)
        return [entry[0], facts] + expand_all(facts, lax.all_to_all(copies, "replica", 0, 0))

    grads = []
    for slot in range(slots):
        active = turn(section, slot, n_section)[1]
        holders = {}
        for holder in range(last + 1):
            chunk = slot - (last - holder)
            if 0 <= chunk < N_CHUNK:
                holders[holder] = chunk
        if slot == 0:
            result, facts, *masks = lax.cond(active, start, rest, entry, relu_mask, route)
        else:
            rows = carried
            if last in holders:
                rows = jnp.where(section == last, entry[holders[last]], rows)
            result = lax.cond(
                active,
                lambda rows, *masks: work(
                    facts, rows, {holder: masks[chunk] for holder, chunk in holders.items()}
                ),
                lambda rows, *masks: rows,
                rows,
                *masks,
            )
        grads.append(result)
        if slot < slots - 1:
            carried = lax.ppermute(result, "section", [(s, s - 1) for s in holders if s > 0])
    outgoing = address(n_section, n_replica, micro, facts, grads)
    got = lax.all_to_all(outgoing, "replica", 0, 0)
    done = jnp.sum(got.astype(jnp.float32), axis=0).astype(jnp.bfloat16)
    return done[None, None]


def solution(mesh):
    in_specs = (
        P("replica", None, "tensor", None),
        P("section", "replica", None, None, "tensor"),
        P("section", None, "tensor"),
        P("section", "tensor", None),
        P(),
    )
    out_specs = P("section", "replica", None, "tensor", None)
    return jax.shard_map(shards, mesh=mesh, in_specs=in_specs, out_specs=out_specs, check_vma=False)
```

```python
import functools

import jax
import jax.numpy as jnp
from jax import lax
from jax.experimental import pallas as pl
from jax.experimental.pallas import tpu as pltpu
from jax.sharding import PartitionSpec as P

N_CHUNK = 2
BLOCK = 1024
COLUMNS = 512
GROUP = BLOCK // 8
MIB = 1024 * 1024
LAST_DIMS = (((1,), (1,)), ((), ()))
SCALARS = pl.BlockSpec(memory_space=pltpu.SMEM)
WHOLE = pl.BlockSpec(memory_space=pltpu.VMEM)
OUTSIDE = pl.BlockSpec(memory_space=pltpu.HBM)


def turn(section, slot, n_section):
    offset = slot - (n_section - 1 - section)
    return jnp.clip(offset, 0, N_CHUNK - 1), (offset >= 0) & (offset < N_CHUNK)


def expand_kernel(chunk, facts_ref, words_ref, out_ref, held_ref, ones_ref, spread_ref, sems):
    sources = words_ref.shape[0]
    micro = held_ref.shape[0]
    parts, rows = out_ref.shape[:2]
    tokens = rows // micro

    def read(m):
        at = chunk * micro + m
        source = 0 if sources == 1 else facts_ref[1 + at]
        return pltpu.make_async_copy(words_ref.at[source, at], held_ref.at[m], sems.at[0, m])

    def write(m):
        place = pl.ds(pl.multiple_of(m * tokens, tokens), tokens)
        return pltpu.make_async_copy(ones_ref.at[m], out_ref.at[:, place], sems.at[1, m])

    for m in range(micro):
        read(m).start()
    word = lax.broadcasted_iota(jnp.int32, spread_ref.shape, 0)
    unit = lax.broadcasted_iota(jnp.int32, spread_ref.shape, 1)
    spread_ref[...] = jnp.where(
        jnp.right_shift(unit, 3) == word, jnp.float32(1), jnp.float32(0)
    ).astype(jnp.bfloat16)
    lane = lax.broadcasted_iota(jnp.int32, (1, BLOCK), 1)
    bit = jnp.left_shift(jnp.int32(1), jnp.bitwise_and(lane, 7))

    @pl.loop(0, micro)
    def _(m):
        read(m).wait()
        for at in range(held_ref.shape[2] // GROUP):
            words = held_ref[m, :, at * GROUP : (at + 1) * GROUP]
            value = jnp.dot(words, spread_ref[...], preferred_element_type=jnp.float32)
            on = jnp.bitwise_and(value.astype(jnp.int32), bit) != 0
            ones = jnp.where(on, jnp.float32(1), jnp.float32(0)).astype(jnp.bfloat16)
            ones_ref[m, :, :, at * BLOCK : (at + 1) * BLOCK] = ones.reshape(parts, tokens, BLOCK)
        write(m).start()

    for m in range(micro):
        write(m).wait()


def expand(chunk, parts, facts, words):
    _, micro, tokens, count = words.shape
    micro //= N_CHUNK
    shape = (parts, micro * tokens // parts, 8 * count)
    return pl.pallas_call(
        functools.partial(expand_kernel, chunk),
        in_specs=[SCALARS, OUTSIDE],
        out_specs=OUTSIDE,
        out_shape=jax.ShapeDtypeStruct(shape, jnp.bfloat16),
        scratch_shapes=[
            pltpu.VMEM((micro, tokens, count), jnp.bfloat16),
            pltpu.VMEM((micro, parts, tokens // parts, 8 * count), jnp.bfloat16),
            pltpu.VMEM((GROUP, BLOCK), jnp.bfloat16),
            pltpu.SemaphoreType.DMA((2, micro)),
        ],
        compiler_params=pltpu.CompilerParams(vmem_limit_bytes=56 * MIB),
        cost_estimate=pl.CostEstimate(
            flops=micro * tokens * count * 8 * 512,
            bytes_accessed=micro * tokens * count * 18,
            transcendentals=0,
        ),
    )(facts, words)


def block_kernel(holders, facts_ref, x_ref, w_out_ref, w_in_ref, *refs):
    mask_refs, refs = refs[: len(holders)], refs[len(holders) :]
    out_ref, w_out_buf, w_in_buf, mask_buf, hidden_ref, sems = refs
    parts, rows, width = x_ref.shape
    total = parts * rows
    n_up, n_down = w_out_ref.shape[0] // BLOCK, width // COLUMNS

    def place(at, size):
        return pl.ds(at * size if isinstance(at, int) else pl.multiple_of(at * size, size), size)

    def up(at):
        units = place(at, BLOCK)
        return pltpu.make_async_copy(w_out_ref.at[units], w_out_buf.at[units], sems.at[0, at])

    def mask(at, ref):
        units = place(at, BLOCK)
        return pltpu.make_async_copy(ref.at[:, :, units], mask_buf.at[:, :, units], sems.at[1, at])

    def down(at):
        columns = place(at, COLUMNS)
        return pltpu.make_async_copy(w_in_ref.at[columns], w_in_buf.at[columns], sems.at[2, at])

    for at in range(n_up):
        up(at).start()
        if len(holders) == 1:
            mask(at, mask_refs[0]).start()
        else:
            for holder, ref in zip(holders, mask_refs):

                @pl.when(facts_ref[0] == holder)
                def _(at=at, ref=ref):
                    mask(at, ref).start()

    for at in range(n_down):
        down(at).start()

    @pl.loop(0, n_up)
    def _(at):
        up(at).wait()
        mask(at, mask_refs[0]).wait()
        units = place(at, BLOCK)
        pre = lax.dot_general(
            x_ref[...].reshape(total, width),
            w_out_buf[units, :],
            LAST_DIMS,
            preferred_element_type=jnp.float32,
        )
        hidden_ref[:, units] = pre.astype(jnp.bfloat16) * mask_buf[:, :, units].reshape(total, BLOCK)

    @pl.loop(0, n_down)
    def _(at):
        down(at).wait()
        columns = place(at, COLUMNS)
        term = lax.dot_general(
            hidden_ref[...], w_in_buf[columns, :], LAST_DIMS, preferred_element_type=jnp.float32
        )
        out_ref[:, :, columns] = term.astype(jnp.bfloat16).reshape(parts, rows, COLUMNS)


def block_sums(facts, x, w_out, w_in, masks):
    parts, rows, width = x.shape
    total = parts * rows
    units = w_out.shape[0]
    return pl.pallas_call(
        functools.partial(block_kernel, tuple(masks)),
        in_specs=[SCALARS, WHOLE] + [OUTSIDE] * (2 + len(masks)),
        out_specs=WHOLE,
        out_shape=jax.ShapeDtypeStruct((parts, rows, width), jnp.bfloat16),
        scratch_shapes=[
            pltpu.VMEM((units, width), jnp.bfloat16),
            pltpu.VMEM((width, units), jnp.bfloat16),
            pltpu.VMEM((parts, rows, units), jnp.bfloat16),
            pltpu.VMEM((total, units), jnp.bfloat16),
            pltpu.SemaphoreType.DMA((3, max(units // BLOCK, width // COLUMNS))),
        ],
        compiler_params=pltpu.CompilerParams(vmem_limit_bytes=52 * MIB),
        cost_estimate=pl.CostEstimate(
            flops=4 * total * width * units, bytes_accessed=4 * width * units, transcendentals=0
        ),
    )(facts, x, w_out, w_in, *masks.values())


def address_kernel(n_section, facts_ref, *refs):
    *grads_refs, out_ref = refs
    n_replica, micro, tokens, _ = out_ref.shape
    per_chunk = micro // N_CHUNK
    for chunk in range(N_CHUNK):
        for section in range(n_section):

            @pl.when(facts_ref[0] == section)
            def _(chunk=chunk, section=section):
                value = grads_refs[chunk + n_section - 1 - section]
                for i in range(per_chunk):
                    m = chunk * per_chunk + i
                    rows = value[i * tokens : (i + 1) * tokens, :]
                    for q in range(n_replica):
                        mine = jnp.where(facts_ref[1 + m] == q, rows, jnp.zeros_like(rows))
                        out_ref[q, m] = mine


def address(n_section, n_replica, micro, facts, grads):
    rows, width = grads[0].shape
    return pl.pallas_call(
        functools.partial(address_kernel, n_section),
        in_specs=[SCALARS] + [WHOLE] * len(grads),
        out_specs=WHOLE,
        out_shape=jax.ShapeDtypeStruct((n_replica, micro, rows * N_CHUNK // micro, width), jnp.bfloat16),
        compiler_params=pltpu.CompilerParams(vmem_limit_bytes=8 * MIB),
    )(facts, *grads)


def shards(out_grad, relu_mask, w_in, w_out, route):
    n_section = lax.axis_size("section")
    n_replica = lax.axis_size("replica")
    n_tensor = lax.axis_size("tensor")
    micro, tokens, width = out_grad.shape[1:]
    section = lax.axis_index("section")
    replica = lax.axis_index("replica")
    per_chunk = micro // N_CHUNK
    last = n_section - 1
    slots = N_CHUNK + last
    w_in_local, w_out_local = w_in[0], w_out[0]
    entry = out_grad[0].reshape(N_CHUNK, per_chunk * tokens, width)
    names = jnp.arange(n_replica, dtype=jnp.int32)

    def facts_of(route):
        belongs = jnp.broadcast_to(replica, (micro,)).astype(jnp.int32)
        for hop in range(last - 1, -1, -1):
            moved = jnp.sum(jnp.where(belongs[:, None] == names, route[hop], 0), axis=1)
            belongs = jnp.where(section <= hop, moved, belongs)
        return jnp.concatenate([section.astype(jnp.int32).reshape(1), belongs])

    def swap(value):
        return lax.all_to_all(value, "tensor", 0, 0)

    def work(facts, rows, masks, sent=None):
        sent = rows if sent is None else sent
        x = swap(jnp.broadcast_to(sent[None], (n_tensor,) + rows.shape))
        partial = block_sums(facts, x, w_out_local, w_in_local, masks)
        total = jnp.sum(swap(partial).astype(jnp.float32), axis=0)
        return (rows.astype(jnp.float32) + total).astype(jnp.bfloat16)

    def expand_all(facts, words):
        return [expand(at, n_tensor, facts, words) for at in range(N_CHUNK)]

    def start(entry, relu_mask, route):
        facts = jnp.where(jnp.arange(1 + micro) == 0, section, replica).astype(jnp.int32)
        masks = expand_all(facts, relu_mask[0].astype(jnp.bfloat16))
        sent, _ = lax.optimization_barrier((entry, section))
        return [work(facts, entry[0], {last: masks[0]}, sent[0]), facts] + masks

    def rest(entry, relu_mask, route):
        words = relu_mask[0, 0].astype(jnp.bfloat16)
        copies = jnp.broadcast_to(words[None], (n_replica,) + words.shape)
        facts = facts_of(route)
        return [entry[0], facts] + expand_all(facts, lax.all_to_all(copies, "replica", 0, 0))

    grads = []
    for slot in range(slots):
        active = turn(section, slot, n_section)[1]
        holders = {}
        for holder in range(last + 1):
            chunk = slot - (last - holder)
            if 0 <= chunk < N_CHUNK:
                holders[holder] = chunk
        if slot == 0:
            result, facts, *masks = lax.cond(active, start, rest, entry, relu_mask, route)
        else:
            rows = carried
            if last in holders:
                rows = jnp.where(section == last, entry[holders[last]], rows)
            result = lax.cond(
                active,
                lambda rows, *masks: work(
                    facts, rows, {holder: masks[chunk] for holder, chunk in holders.items()}
                ),
                lambda rows, *masks: rows,
                rows,
                *masks,
            )
        grads.append(result)
        if slot < slots - 1:
            carried = lax.ppermute(result, "section", [(s, s - 1) for s in holders if s > 0])
    outgoing = address(n_section, n_replica, micro, facts, grads)
    got = lax.all_to_all(outgoing, "replica", 0, 0)
    done = jnp.sum(got.astype(jnp.float32), axis=0).astype(jnp.bfloat16)
    return done[None, None]


def solution(mesh):
    in_specs = (
        P("replica", None, "tensor", None),
        P("section", "replica", None, None, "tensor"),
        P("section", None, "tensor"),
        P("section", "tensor", None),
        P(),
    )
    out_specs = P("section", "replica", None, "tensor", None)
    return jax.shard_map(shards, mesh=mesh, in_specs=in_specs, out_specs=out_specs, check_vma=False)
```
